32 devices in a mesh: dp: 16 (over z, y, x), tensor: 2 (over core).
Axes of the slice: x: 2, y: 2, z: 4, core: 2. Of those that a mesh axis runs over, the one named last changes fastest.
Arguments:
- queries: bfloat16 [12288, 8192], P('dp', 'tensor'), may hold values from -170 to 170
- key_value_pairs: bfloat16 [12288, 2, 1024], P('dp', None, 'tensor'), may hold values from -6 to 6
- document_numbers: int32 [12288], P('dp'), may hold values from 0 to 11, as said below
- destinations: int32 [16, 12], P('dp'), may hold values from 0 to 15, as said below
- adapter_down_weight: bfloat16 [8192, 64], P('tensor'), may hold values from -0.0625 to 0.0625
- adapter_up_weight: bfloat16 [64, 5120], P(None, 'tensor'), may hold values from -0.75 to 0.75
- cotangent: bfloat16 [12288, 5120], P('dp', 'tensor'), may hold values from -6 to 6
Outputs:
- arrived_out: bfloat16 [4096, 8192], P('dp', 'tensor')
- adapter_output: bfloat16 [12288, 5120], P('dp', 'tensor')
- grad_down: float32 [8192, 64], P('tensor')
- grad_up: float32 [64, 5120], P(None, 'tensor')
The draws below stay inside these ranges and needn't reach their ends.
Inputs may be any that keep to these rules, and one draw needn't show every extreme that they name: `document_numbers`: within each replica's 768 rows the ids never fall and rise by one from 0 to 11: every document holds one or more consecutive rows. destinations[r, j] is the replica that takes document j of replica r. For each k from 1 to 4, exactly one document of every replica r goes to replica r XOR (16 / 2**k) (bitwise exclusive or); the other 8 stay (destination r). A document that leaves holds at most 64 rows, and every replica sends one of exactly 64 rows.
All inputs are finite; a program needn't handle non-finite values.
Results may differ from the reference program's by a relative error of at most 0.0062.
Values may be sent and summed in bfloat16 or wider, within the bound.
A program may use at most 64 MiB of HBM per device.

```python
import math
import jax
import jax.numpy as jnp
from jax import lax

MODEL_WIDTH = 5120
QUERY_HEAD_COUNT = 64
KEY_VALUE_HEADS = 8
HEAD_SIZE = 128
ADAPTER_RANK = 64
REPLICA_TOKENS = 768
NDOC = 12
MOVES = 4
CAP = 64
REPLICA_COUNT = 16
TOKEN_TOTAL = 12288
ARRIVED = 4096


def attention_rows(key):
    rows_of_keys = jnp.clip(jax.random.normal(jax.random.fold_in(key, 101), (TOKEN_TOTAL, KEY_VALUE_HEADS * HEAD_SIZE), jnp.float32), -6.0, 6.0)
    return rows_of_keys


def documents(key):
    doc_ids = jnp.arange(NDOC, dtype=jnp.int32)
    scores = jax.random.randint(jax.random.fold_in(key, 201), (REPLICA_COUNT, NDOC), 0, 1 << 20, dtype=jnp.int32) * NDOC + doc_ids
    doc_rank = jnp.argsort(jnp.argsort(scores, axis=1), axis=1).astype(jnp.int32)
    leaving = jax.random.randint(jax.random.fold_in(key, 202), (REPLICA_COUNT, MOVES), CAP // 4, CAP + 1, dtype=jnp.int32)
    full_slot = jax.random.randint(jax.random.fold_in(key, 203), (REPLICA_COUNT, 1), 0, MOVES, dtype=jnp.int32)
    leaving = jnp.where(jnp.arange(MOVES, dtype=jnp.int32)[None, :] == full_slot, CAP, leaving)
    remaining = REPLICA_TOKENS - jnp.sum(leaving, axis=1)
    spare = remaining - (NDOC - MOVES)
    cut_points = jax.random.randint(jax.random.fold_in(key, 204), (REPLICA_COUNT, NDOC - MOVES - 1), 0, spare[:, None] + 1, dtype=jnp.int32)
    cut_points = jnp.sort(cut_points, axis=1)
    bounds = jnp.concatenate([jnp.zeros((REPLICA_COUNT, 1), jnp.int32), cut_points, spare[:, None]], axis=1)
    staying_lengths = jnp.diff(bounds, axis=1) + 1
    length_pool = jnp.concatenate([leaving, staying_lengths], axis=1)
    lengths = jnp.take_along_axis(length_pool, doc_rank, axis=1)
    ends = jnp.cumsum(lengths, axis=1)
    position = jnp.arange(REPLICA_TOKENS, dtype=jnp.int32)
    segments = jnp.sum((position[None, :, None] >= ends[:, None, :]).astype(jnp.int32), axis=2)
    replica = jnp.arange(REPLICA_COUNT, dtype=jnp.int32)[:, None]
    distance = jnp.right_shift(jnp.int32(REPLICA_COUNT), jnp.minimum(doc_rank, MOVES - 1) + 1)
    destination = jnp.where(doc_rank < MOVES, jnp.bitwise_xor(replica, distance), replica)
    return (segments.reshape(TOKEN_TOTAL).astype(jnp.int32), destination.astype(jnp.int32))


def draw_queries(key, part):
    key = jax.random.fold_in(key, 1)
    own_rows = jnp.clip(jax.random.normal(key, (TOKEN_TOTAL, QUERY_HEAD_COUNT * HEAD_SIZE), jnp.float32), -6.0, 6.0)
    return own_rows.astype(jnp.bfloat16)


def draw_key_value_pairs(key, part):
    rows_of_keys = attention_rows(key)
    key = jax.random.fold_in(key, 2)
    rows_of_values = jnp.clip(jax.random.normal(key, (TOKEN_TOTAL, KEY_VALUE_HEADS * HEAD_SIZE), jnp.float32), -6.0, 6.0)
    return jnp.stack([rows_of_keys, rows_of_values], axis=1).astype(jnp.bfloat16)


def draw_document_numbers(key, part):
    segments, destination = documents(key)
    return segments


def draw_destinations(key, part):
    segments, destination = documents(key)
    return destination


def levels(rng, dims, cuts, smallest, largest):
    level, own = 1.0, jax.random.fold_in(rng, 6)
    for axis_at, blocks in cuts:
        heights = jnp.exp(jax.random.uniform(jax.random.fold_in(own, axis_at), (blocks,), jnp.float32, smallest / len(cuts), largest / len(cuts)))
        level = level * jnp.repeat(heights, dims[axis_at] // blocks).reshape([-1 if axis == axis_at else 1 for axis in range(len(dims))])
    return level


def centred(rng, extent, width, reach, cuts=(), kind=jnp.bfloat16):
    result = width * jax.random.normal(rng, extent, jnp.float32)
    if cuts:
        result = result * levels(rng, extent, cuts, -0.22, 0.18)
    return jnp.clip(result, -reach, reach).astype(kind)


def setup_inputs(seed: int = 0) -> dict:
    streams_of = jax.random.split(jax.random.key(seed), 8)
    return {
        "queries": draw_queries(jax.random.fold_in(streams_of[7], 71), 0),
        "key_value_pairs": draw_key_value_pairs(jax.random.fold_in(streams_of[7], 71), 0),
        "document_numbers": draw_document_numbers(jax.random.fold_in(streams_of[7], 71), 0),
        "destinations": draw_destinations(jax.random.fold_in(streams_of[7], 71), 0),
        "adapter_down_weight": centred(streams_of[4], (QUERY_HEAD_COUNT * HEAD_SIZE, ADAPTER_RANK), (QUERY_HEAD_COUNT * HEAD_SIZE) ** -0.5, 0.0625, ((0, 2),)),
        "adapter_up_weight": centred(streams_of[5], (ADAPTER_RANK, MODEL_WIDTH), ADAPTER_RANK ** -0.5, 0.75, ((1, 2),)),
        "cotangent": centred(streams_of[6], (TOKEN_TOTAL, MODEL_WIDTH), 1.0, 6.0, ((0, 16), (1, 2))),
    }


ADAPTER_SCALE = 2.0
MASKED_SCORE = -1e+30

def attend_head(query_head, key_head, value_head, allowed):
    scores = lax.dot_general(query_head, key_head, (((1,), (1,)), ((), ())), preferred_element_type=jnp.float32) * HEAD_SIZE ** (-0.5)
    scores = jnp.where(allowed, scores, MASKED_SCORE)
    row_max = lax.optimization_barrier(jnp.max(scores, axis=1, keepdims=True))
    weights = jnp.where(allowed, jnp.exp(scores - row_max), 0.0)
    probabilities = (weights / lax.optimization_barrier(jnp.sum(weights, axis=1, keepdims=True))).astype(jnp.bfloat16)
    return jnp.dot(probabilities, value_head, preferred_element_type=jnp.float32).astype(jnp.bfloat16)

def attention_per_replica(operands):
    query_rows, paired_rows, segment = operands
    position = jnp.arange(REPLICA_TOKENS)
    allowed = (segment[:, None] == segment[None, :]) & (position[:, None] >= position[None, :])
    query_heads = query_rows.reshape(REPLICA_TOKENS, QUERY_HEAD_COUNT, HEAD_SIZE).transpose(1, 0, 2)
    heads_of_keys = paired_rows[:, 0].reshape(REPLICA_TOKENS, KEY_VALUE_HEADS, HEAD_SIZE).transpose(1, 0, 2)
    heads_of_values = paired_rows[:, 1].reshape(REPLICA_TOKENS, KEY_VALUE_HEADS, HEAD_SIZE).transpose(1, 0, 2)
    query_group_size = QUERY_HEAD_COUNT // KEY_VALUE_HEADS

    def one_head(head_index):
        return attend_head(query_heads[head_index], heads_of_keys[head_index // query_group_size], heads_of_values[head_index // query_group_size], allowed)
    head_outputs = lax.map(one_head, jnp.arange(QUERY_HEAD_COUNT))
    return head_outputs.transpose(1, 0, 2).reshape(REPLICA_TOKENS, QUERY_HEAD_COUNT * HEAD_SIZE)

def reference(queries, key_value_pairs, document_numbers, destinations, adapter_down_weight, adapter_up_weight, cotangent):
    attention_layer = lax.map(attention_per_replica, (queries.reshape(REPLICA_COUNT, REPLICA_TOKENS, QUERY_HEAD_COUNT * HEAD_SIZE), key_value_pairs.reshape(REPLICA_COUNT, REPLICA_TOKENS, 2, KEY_VALUE_HEADS * HEAD_SIZE), document_numbers.reshape(REPLICA_COUNT, REPLICA_TOKENS)))
    attention_layer = attention_layer.reshape(TOKEN_TOTAL, QUERY_HEAD_COUNT * HEAD_SIZE)
    adapter_hidden = jnp.dot(attention_layer, adapter_down_weight, preferred_element_type=jnp.float32).astype(jnp.bfloat16)
    adapter_output = (ADAPTER_SCALE * jnp.dot(adapter_hidden, adapter_up_weight, preferred_element_type=jnp.float32)).astype(jnp.bfloat16)
    feedback_signal = lax.dot_general(cotangent, adapter_up_weight, (((1,), (1,)), ((), ())), preferred_element_type=jnp.float32).astype(jnp.bfloat16)
    gradient_scale = ADAPTER_SCALE / math.sqrt(TOKEN_TOTAL)
    grad_down = gradient_scale * lax.dot_general(attention_layer, feedback_signal, (((0,), (0,)), ((), ())), preferred_element_type=jnp.float32)
    grad_up = gradient_scale * lax.dot_general(adapter_hidden, cotangent, (((0,), (0,)), ((), ())), preferred_element_type=jnp.float32)
    doc_ids = jnp.arange(NDOC, dtype=jnp.int32)
    segments = document_numbers.reshape(REPLICA_COUNT, REPLICA_TOKENS)
    lengths = lax.optimization_barrier(jnp.sum((segments[:, :, None] == doc_ids).astype(jnp.int32), axis=1))
    starts = lax.optimization_barrier(jnp.sum((segments[:, :, None] < doc_ids).astype(jnp.int32), axis=1))
    receiver = jnp.arange(REPLICA_COUNT, dtype=jnp.int32)[:, None]
    distance = jnp.array([REPLICA_COUNT >> slot + 1 for slot in range(MOVES)], dtype=jnp.int32)
    source = jnp.bitwise_xor(receiver, distance[None, :])
    sent = destinations[source] == receiver[:, :, None]
    picked = lax.optimization_barrier(jnp.sum(jnp.where(sent, doc_ids, 0), axis=2)).astype(jnp.int32)
    start = jnp.take_along_axis(starts[source], picked[:, :, None], axis=2)[:, :, 0]
    length = jnp.take_along_axis(lengths[source], picked[:, :, None], axis=2)[:, :, 0]
    offsets = jnp.arange(CAP, dtype=jnp.int32)
    live_rows = offsets[None, None, :] < length[:, :, None]
    row_index = (source[:, :, None] * REPLICA_TOKENS + jnp.minimum(start[:, :, None] + offsets[None, None, :], REPLICA_TOKENS - 1)).astype(jnp.int32)
    gathered = attention_layer[row_index.reshape(ARRIVED)]
    arrived_out = jnp.where(live_rows.reshape(ARRIVED)[:, None], gathered, jnp.zeros_like(gathered))
    return (arrived_out, adapter_output, grad_down, grad_up)
```

```python
import functools
import math

import jax
import jax.numpy as jnp
from jax import lax
from jax.experimental import pallas as pl
from jax.experimental.pallas import tpu as pltpu
from jax.sharding import PartitionSpec as P

HEAD_SIZE = 128
NDOC = 12
MOVES = 4
CAP = 64
TILE = 128
HEADS_PER_DOT = 4

ADAPTER_SCALE = 2.0
MASKED_SCORE = -1e30
EXP2_SCALE = HEAD_SIZE ** (-0.5) * math.log2(math.e)


def from_partner(value, axis, apart):
    mask = 2**apart
    pairs = [(source, source ^ mask) for source in range(lax.axis_size(axis))]
    return lax.ppermute(value, axis, pairs)


def attention_kernel(
    gradient_scale, tiles_ref, query_ref, key_ref, value_ref, doc_col_ref, doc_row_ref, target_ref,
    down_ref, feedback_ref, outgoing_ref, hidden_ref, grad_ref, attention_ref,
):
    group, block = pl.program_id(0), pl.program_id(1)
    blocks = attention_ref.shape[0] // TILE
    heads = query_ref.shape[1] // HEAD_SIZE

    def attend(count):
        width = count * TILE
        start = pl.multiple_of((block + 1 - count) * TILE, TILE)
        keys = key_ref[pl.ds(start, width), :]
        values = jnp.concatenate(
            [value_ref[pl.ds(start, width), :], jnp.ones((width, HEAD_SIZE), jnp.bfloat16)], axis=1
        )
        rows = lax.broadcasted_iota(jnp.int32, (TILE, width), 0) + block * TILE
        columns = lax.broadcasted_iota(jnp.int32, (TILE, width), 1) + start
        same = doc_col_ref[...] == doc_row_ref[:, pl.ds(start, width)]
        bias = jnp.where(same & (rows >= columns), 0.0, MASKED_SCORE)
        for first in range(0, heads, HEADS_PER_DOT):
            picked = range(first, min(first + HEADS_PER_DOT, heads))
            stacked = jnp.concatenate(
                [query_ref[:, h * HEAD_SIZE : (h + 1) * HEAD_SIZE] for h in picked], axis=0
            )
            scores = lax.dot_general(
                stacked, keys, (((1,), (1,)), ((), ())), preferred_element_type=jnp.float32
            )
            scores = scores.reshape(len(picked), TILE, width) * EXP2_SCALE + bias[None]
            row_max = jnp.max(scores, axis=2, keepdims=True)
            weights = jnp.exp2(scores - row_max).astype(jnp.bfloat16)
            product = jnp.dot(
                weights.reshape(len(picked) * TILE, width), values,
                preferred_element_type=jnp.float32,
            )
            result = (product[:, :HEAD_SIZE] / product[:, HEAD_SIZE:]).astype(jnp.bfloat16)
            for at, h in enumerate(picked):
                attention_ref[
                    pl.ds(pl.multiple_of(block * TILE, TILE), TILE),
                    h * HEAD_SIZE : (h + 1) * HEAD_SIZE,
                ] = result[at * TILE : (at + 1) * TILE]

    for count in range(1, blocks + 1):
        pl.when(tiles_ref[block] == count)(functools.partial(attend, count))

    @pl.when(block == blocks - 1)
    def _():
        attention = attention_ref[...]
        moved = lax.broadcasted_iota(jnp.int32, (MOVES * CAP, attention.shape[0]), 1)
        pick = jnp.where(moved == target_ref[...], 1.0, 0.0).astype(jnp.bfloat16)
        outgoing_ref[...] = jnp.dot(
            pick, attention, preferred_element_type=jnp.float32
        ).astype(jnp.bfloat16)
        part = jnp.dot(attention, down_ref[...], preferred_element_type=jnp.float32)

        @pl.when(group == 0)
        def _():
            hidden_ref[...] = part

        @pl.when(group > 0)
        def _():
            hidden_ref[...] += part

        grad_ref[...] = gradient_scale * jnp.dot(
            feedback_ref[...], attention, preferred_element_type=jnp.float32
        )


def attend_all(
    queries, keys, values, documents, tiles, targets, down_weight, feedback, gradient_scale
):
    rows, features = queries.shape
    groups = keys.shape[1] // HEAD_SIZE
    width = features // groups
    rank = down_weight.shape[1]
    blocks = rows // TILE
    grid_spec = pltpu.PrefetchScalarGridSpec(
        num_scalar_prefetch=1,
        grid=(groups, blocks),
        in_specs=[
            pl.BlockSpec((TILE, width), lambda g, i, t: (i, g)),
            pl.BlockSpec((rows, HEAD_SIZE), lambda g, i, t: (0, g)),
            pl.BlockSpec((rows, HEAD_SIZE), lambda g, i, t: (0, g)),
            pl.BlockSpec((TILE, 1), lambda g, i, t: (i, 0)),
            pl.BlockSpec((1, rows), lambda g, i, t: (0, 0)),
            pl.BlockSpec((MOVES * CAP, 1), lambda g, i, t: (0, 0)),
            pl.BlockSpec((width, rank), lambda g, i, t: (g, 0)),
            pl.BlockSpec((rank, rows), lambda g, i, t: (0, 0)),
        ],
        out_specs=[
            pl.BlockSpec((MOVES * CAP, width), lambda g, i, t: (0, g)),
            pl.BlockSpec((rows, rank), lambda g, i, t: (0, 0)),
            pl.BlockSpec((rank, width), lambda g, i, t: (0, g)),
        ],
        scratch_shapes=[pltpu.VMEM((rows, width), jnp.bfloat16)],
    )
    return pl.pallas_call(
        functools.partial(attention_kernel, gradient_scale),
        grid_spec=grid_spec,
        out_shape=[
            jax.ShapeDtypeStruct((MOVES * CAP, features), jnp.bfloat16),
            jax.ShapeDtypeStruct((rows, rank), jnp.float32),
            jax.ShapeDtypeStruct((rank, features), jnp.float32),
        ],
        compiler_params=pltpu.CompilerParams(vmem_limit_bytes=40 * 2**20),
        cost_estimate=pl.CostEstimate(
            flops=3 * rows * rows * features, bytes_accessed=4 * rows * features,
            transcendentals=rows * rows * features // (2 * HEAD_SIZE),
        ),
    )(
        tiles, queries, keys, values, documents[:, None], documents[None, :], targets[:, None],
        down_weight, feedback,
    )


def on_device(
    queries,
    key_value_pairs,
    document_numbers,
    destinations,
    adapter_down_weight,
    adapter_up_weight,
    cotangent,
):
    token_rows = queries.shape[0]
    replica_list = lax.axis_size("dp")
    own_index = lax.axis_index("dp")
    top_bit = replica_list.bit_length() - 1
    gradient_scale = ADAPTER_SCALE / math.sqrt(token_rows * replica_list)
    partial_feedback = lax.dot_general(
        adapter_up_weight, cotangent, (((1,), (1,)), ((), ())), preferred_element_type=jnp.float32
    )
    feedback_signal = lax.psum(partial_feedback, "tensor").astype(jnp.bfloat16)

    doc_ids = jnp.arange(NDOC, dtype=jnp.int32)
    lengths = jnp.sum((document_numbers[:, None] == doc_ids).astype(jnp.int32), axis=0)
    starts = jnp.sum((document_numbers[:, None] < doc_ids).astype(jnp.int32), axis=0)
    partners = jnp.bitwise_xor(
        own_index, jnp.array([replica_list >> k + 1 for k in range(MOVES)], jnp.int32)
    )
    chosen = destinations[0][None, :] == partners[:, None]
    sent_start = jnp.sum(jnp.where(chosen, starts, 0), axis=1)
    sent_length = jnp.sum(jnp.where(chosen, lengths, 0), axis=1)
    offsets = jnp.arange(CAP, dtype=jnp.int32)[None, :]
    targets = jnp.where(
        offsets < sent_length[:, None], sent_start[:, None] + offsets, -1
    ).reshape(MOVES * CAP)
    blocks = token_rows // TILE
    first_document = document_numbers.reshape(blocks, TILE)[:, 0]
    first_row = jnp.sum(
        (document_numbers[None, :] < first_document[:, None]).astype(jnp.int32), axis=1
    )
    tiles = jnp.arange(1, blocks + 1, dtype=jnp.int32) - first_row // TILE

    outgoing, hidden_part, grad_down_part = attend_all(
        queries, key_value_pairs[:, 0], key_value_pairs[:, 1], document_numbers, tiles, targets,
        adapter_down_weight, feedback_signal, gradient_scale,
    )
    arrived = [
        from_partner(outgoing[slot * CAP : (slot + 1) * CAP], "dp", top_bit - 1 - slot)
        for slot in range(MOVES)
    ]
    arrived_out = jnp.concatenate(arrived, axis=0)
    adapter_hidden = lax.psum(hidden_part, "tensor").astype(jnp.bfloat16)
    adapter_output = (
        ADAPTER_SCALE
        * jnp.dot(adapter_hidden, adapter_up_weight, preferred_element_type=jnp.float32)
    ).astype(jnp.bfloat16)
    grad_up_part = gradient_scale * lax.dot_general(
        adapter_hidden, cotangent, (((0,), (0,)), ((), ())), preferred_element_type=jnp.float32
    )
    grad_down, grad_up = lax.psum((grad_down_part, grad_up_part), "dp")
    return (arrived_out, adapter_output, grad_down.T, grad_up)


def solution(mesh):
    placed = (
        P("dp", "tensor"),
        P("dp", None, "tensor"),
        P("dp"),
        P("dp", None),
        P("tensor", None),
        P(None, "tensor"),
        P("dp", "tensor"),
    )
    return jax.shard_map(
        on_device,
        mesh=mesh,
        in_specs=placed,
        out_specs=(P("dp", "tensor"), P("dp", "tensor"), P("tensor", None), P(None, "tensor")),
        check_vma=False,
    )
```

```python
import functools
import math

import jax
import jax.numpy as jnp
from jax import lax
from jax.experimental import pallas as pl
from jax.experimental.pallas import tpu as pltpu
from jax.sharding import PartitionSpec as P

HEAD_SIZE = 128
NDOC = 12
MOVES = 4
CAP = 64
TILE = 128
HEADS_PER_DOT = 4

ADAPTER_SCALE = 2.0
MASKED_SCORE = -1e30
EXP2_SCALE = HEAD_SIZE ** (-0.5) * math.log2(math.e)


def attention_kernel(
    gradient_scale, tiles_ref, query_ref, key_ref, value_ref, doc_col_ref, doc_row_ref, target_ref,
    down_ref, feedback_ref, outgoing_ref, hidden_ref, grad_ref, attention_ref,
):
    group, block = pl.program_id(0), pl.program_id(1)
    blocks = attention_ref.shape[0] // TILE
    heads = query_ref.shape[1] // HEAD_SIZE

    def attend(count):
        width = count * TILE
        start = pl.multiple_of((block + 1 - count) * TILE, TILE)
        keys = key_ref[pl.ds(start, width), :]
        values = jnp.concatenate(
            [value_ref[pl.ds(start, width), :], jnp.ones((width, HEAD_SIZE), jnp.bfloat16)], axis=1
        )
        rows = lax.broadcasted_iota(jnp.int32, (TILE, width), 0) + block * TILE
        columns = lax.broadcasted_iota(jnp.int32, (TILE, width), 1) + start
        same = doc_col_ref[...] == doc_row_ref[:, pl.ds(start, width)]
        bias = jnp.where(same & (rows >= columns), 0.0, MASKED_SCORE)
        for first in range(0, heads, HEADS_PER_DOT):
            picked = range(first, min(first + HEADS_PER_DOT, heads))
            stacked = jnp.concatenate(
                [query_ref[:, h * HEAD_SIZE : (h + 1) * HEAD_SIZE] for h in picked], axis=0
            )
            scores = lax.dot_general(
                stacked, keys, (((1,), (1,)), ((), ())), preferred_element_type=jnp.float32
            )
            scores = scores.reshape(len(picked), TILE, width) * EXP2_SCALE + bias[None]
            row_max = jnp.max(scores, axis=2, keepdims=True)
            weights = jnp.exp2(scores - row_max).astype(jnp.bfloat16)
            product = jnp.dot(
                weights.reshape(len(picked) * TILE, width), values,
                preferred_element_type=jnp.float32,
            )
            result = (product[:, :HEAD_SIZE] / product[:, HEAD_SIZE:]).astype(jnp.bfloat16)
            for at, h in enumerate(picked):
                attention_ref[
                    pl.ds(pl.multiple_of(block * TILE, TILE), TILE),
                    h * HEAD_SIZE : (h + 1) * HEAD_SIZE,
                ] = result[at * TILE : (at + 1) * TILE]

    for count in range(1, blocks + 1):
        pl.when(tiles_ref[block] == count)(functools.partial(attend, count))

    @pl.when(block == blocks - 1)
    def _():
        attention = attention_ref[...]
        moved = lax.broadcasted_iota(jnp.int32, (MOVES * CAP, attention.shape[0]), 1)
        pick = jnp.where(moved == target_ref[...], 1.0, 0.0).astype(jnp.bfloat16)
        outgoing_ref[...] = jnp.dot(
            pick, attention, preferred_element_type=jnp.float32
        ).astype(jnp.bfloat16)
        part = jnp.dot(attention, down_ref[...], preferred_element_type=jnp.float32)

        @pl.when(group == 0)
        def _():
            hidden_ref[...] = part

        @pl.when(group > 0)
        def _():
            hidden_ref[...] += part

        grad_ref[...] = gradient_scale * jnp.dot(
            feedback_ref[...], attention, preferred_element_type=jnp.float32
        )


def attend_all(
    queries, keys, values, documents, tiles, targets, down_weight, feedback, gradient_scale
):
    rows, features = queries.shape
    groups = keys.shape[1] // HEAD_SIZE
    width = features // groups
    rank = down_weight.shape[1]
    blocks = rows // TILE
    grid_spec = pltpu.PrefetchScalarGridSpec(
        num_scalar_prefetch=1,
        grid=(groups, blocks),
        in_specs=[
            pl.BlockSpec((TILE, width), lambda g, i, t: (i, g)),
            pl.BlockSpec((rows, HEAD_SIZE), lambda g, i, t: (0, g)),
            pl.BlockSpec((rows, HEAD_SIZE), lambda g, i, t: (0, g)),
            pl.BlockSpec((TILE, 1), lambda g, i, t: (i, 0)),
            pl.BlockSpec((1, rows), lambda g, i, t: (0, 0)),
            pl.BlockSpec((MOVES * CAP, 1), lambda g, i, t: (0, 0)),
            pl.BlockSpec((width, rank), lambda g, i, t: (g, 0)),
            pl.BlockSpec((rank, rows), lambda g, i, t: (0, 0)),
        ],
        out_specs=[
            pl.BlockSpec((MOVES * CAP, width), lambda g, i, t: (0, g)),
            pl.BlockSpec((rows, rank), lambda g, i, t: (0, 0)),
            pl.BlockSpec((rank, width), lambda g, i, t: (0, g)),
        ],
        scratch_shapes=[pltpu.VMEM((rows, width), jnp.bfloat16)],
    )
    return pl.pallas_call(
        functools.partial(attention_kernel, gradient_scale),
        grid_spec=grid_spec,
        out_shape=[
            jax.ShapeDtypeStruct((MOVES * CAP, features), jnp.bfloat16),
            jax.ShapeDtypeStruct((rows, rank), jnp.float32),
            jax.ShapeDtypeStruct((rank, features), jnp.float32),
        ],
        compiler_params=pltpu.CompilerParams(vmem_limit_bytes=40 * 2**20),
        cost_estimate=pl.CostEstimate(
            flops=3 * rows * rows * features, bytes_accessed=4 * rows * features,
            transcendentals=rows * rows * features // (2 * HEAD_SIZE),
        ),
    )(
        tiles, queries, keys, values, documents[:, None], documents[None, :], targets[:, None],
        down_weight, feedback,
    )


def exchange_kernel(
    sizes, gradient_scale, outgoing_ref, hidden_ref, down_part_ref, up_ref, cotangent_ref,
    arrived_ref, output_ref, grad_down_ref, grad_up_ref,
    hidden_in, parts0, parts1, near0, near1, sums0, sums1, far0, far1, whole0, whole1,
    move_send, move_recv, hidden_send, hidden_recv, near_send, near_recv, far_send, far_recv,
    back_send, back_recv, full_send, full_recv,
):
    near, far, cores, lanes = sizes
    replicas = near * far
    own = lax.axis_index("dp")
    core = lax.axis_index("tensor")
    mine, level = lax.rem(own, near), own // near
    columns_out = output_ref.shape[1]

    def near_peer(step):
        return lax.rem(mine + step, near)

    def far_peer(step):
        return lax.rem(level + step, far)

    def at_near(step):
        return {"dp": level * near + near_peer(step)}

    def at_far(step):
        return {"dp": far_peer(step) * near + mine}

    def at_core(step):
        return {"tensor": lax.rem(core + step, cores)}

    devices = [at_near(d) for d in range(1, near)] + [at_far(d) for d in range(1, far)]
    devices += [at_core(d) for d in range(1, cores)]
    barrier = pltpu.get_barrier_semaphore()
    for device in devices:
        pl.semaphore_signal(barrier, inc=1, device_id=device, device_id_type=pl.DeviceIdType.MESH)
    pl.semaphore_wait(barrier, len(devices))

    started = []

    def send(source, target, send_sem, recv_sem, device):
        copy = pltpu.make_async_remote_copy(
            src_ref=source, dst_ref=target, send_sem=send_sem, recv_sem=recv_sem,
            device_id=device, device_id_type=pl.DeviceIdType.MESH,
        )
        copy.start()
        started.append(copy)
        return copy

    hidden_copies = [
        send(hidden_ref, hidden_in.at[d], hidden_send.at[d], hidden_recv.at[d], at_core(d))
        for d in range(1, cores)
    ]

    def fill(parts, value):
        width = parts.shape[3]
        for chunk in range(replicas):
            row, lane = chunk // lanes, chunk % lanes
            have = max(0, min(width, value.shape[1] - lane * width))
            slot = parts.at[chunk // far, chunk % far]
            if have < width:
                slot[...] = jnp.zeros((16, width), jnp.bfloat16)
            if have:
                slot[:, :have] = value[
                    row * 16 : (row + 1) * 16, lane * width : lane * width + have
                ].astype(jnp.bfloat16)

    def scatter_near(at, parts, arrivals):
        return [
            send(
                parts.at[near_peer(d)], arrivals.at[d], near_send.at[at, d], near_recv.at[at, d],
                at_near(d),
            )
            for d in range(1, near)
        ]

    fill(parts0, down_part_ref)
    near_copies0 = scatter_near(0, parts0, near0)

    move_copies = []
    for k in range(MOVES):
        bit = replicas >> k + 1
        partner = own + bit - 2 * bit * lax.rem(own // bit, 2)
        rows = pl.ds(k * CAP, CAP)
        move_copies.append(
            send(
                outgoing_ref.at[rows], arrived_ref.at[rows], move_send.at[k], move_recv.at[k],
                {"dp": partner},
            )
        )

    total = hidden_ref[...]
    for d, copy in enumerate(hidden_copies):
        copy.wait_recv()
        total = total + hidden_in[d + 1]
    hidden = total.astype(jnp.bfloat16)
    hidden_turned = total.T.astype(jnp.bfloat16)
    fill(
        parts1,
        gradient_scale
        * jnp.dot(hidden_turned, cotangent_ref[...], preferred_element_type=jnp.float32),
    )
    near_copies1 = scatter_near(1, parts1, near1)

    step = 640 if columns_out % 640 == 0 else 128
    for first in range(0, columns_out, step):
        output_ref[:, first : first + step] = (
            ADAPTER_SCALE
            * jnp.dot(
                hidden, up_ref[:, first : first + step], preferred_element_type=jnp.float32
            )
        ).astype(jnp.bfloat16)

    def sum_near(copies, parts, arrivals, sums):
        value = parts[mine].astype(jnp.float32)
        for d, copy in enumerate(copies):
            copy.wait_recv()
            value = value + arrivals[d + 1].astype(jnp.float32)
        sums[...] = value.astype(jnp.bfloat16)

    def scatter_far(at, sums, arrivals):
        return [
            send(
                sums.at[far_peer(d)], arrivals.at[d], far_send.at[at, d], far_recv.at[at, d],
                at_far(d),
            )
            for d in range(1, far)
        ]

    def sum_far(copies, sums, arrivals, whole):
        value = sums[level].astype(jnp.float32)
        for d, copy in enumerate(copies):
            copy.wait_recv()
            value = value + arrivals[d + 1].astype(jnp.float32)
        whole[mine, level] = value.astype(jnp.bfloat16)

    def gather_far(at, whole):
        return [
            send(
                whole.at[mine, level], whole.at[mine, level], back_send.at[at, d],
                back_recv.at[at, d], at_far(d),
            )
            for d in range(1, far)
        ]

    def gather_near(at, copies, whole):
        for copy in copies:
            copy.wait_recv()
        return [
            send(
                whole.at[mine], whole.at[mine], full_send.at[at, d], full_recv.at[at, d],
                at_near(d),
            )
            for d in range(1, near)
        ]

    def give(copies, whole, target):
        for copy in copies:
            copy.wait_recv()
        width = whole.shape[3]
        for chunk in range(replicas):
            row, lane = chunk // lanes, chunk % lanes
            have = max(0, min(width, target.shape[1] - lane * width))
            if have:
                target[row * 16 : (row + 1) * 16, lane * width : lane * width + have] = whole[
                    chunk // far, chunk % far
                ][:, :have].astype(jnp.float32)

    sum_near(near_copies0, parts0, near0, sums0)
    far_copies0 = scatter_far(0, sums0, far0)
    sum_near(near_copies1, parts1, near1, sums1)
    far_copies1 = scatter_far(1, sums1, far1)
    sum_far(far_copies0, sums0, far0, whole0)
    back_copies0 = gather_far(0, whole0)
    sum_far(far_copies1, sums1, far1, whole1)
    back_copies1 = gather_far(1, whole1)
    full_copies0 = gather_near(0, back_copies0, whole0)
    full_copies1 = gather_near(1, back_copies1, whole1)
    give(full_copies0, whole0, grad_down_ref)
    give(full_copies1, whole1, grad_up_ref)
    for copy in move_copies:
        copy.wait_recv()
    for copy in started:
        copy.wait_send()


def exchange(outgoing, hidden_part, grad_down_part, up_weight, cotangent, gradient_scale):
    replicas, cores = lax.axis_size("dp"), lax.axis_size("tensor")
    near = 1 << replicas.bit_length() // 2
    far = replicas // near
    rank, features = grad_down_part.shape
    columns = cotangent.shape[1]
    lanes = replicas * 16 // rank
    widths = [-(-size // (lanes * 128)) * 128 for size in (features, columns)]

    def pieces(*lead):
        return [pltpu.VMEM((*lead, 16, width), jnp.bfloat16) for width in widths]

    def semaphores(*shape):
        return [pltpu.SemaphoreType.DMA(shape), pltpu.SemaphoreType.DMA(shape)]

    vmem = pl.BlockSpec(memory_space=pltpu.VMEM)
    hbm = pl.BlockSpec(memory_space=pl.ANY)
    return pl.pallas_call(
        functools.partial(exchange_kernel, (near, far, cores, lanes), gradient_scale),
        in_specs=[hbm, vmem, vmem, vmem, vmem],
        out_specs=[hbm, vmem, vmem, vmem],
        out_shape=[
            jax.ShapeDtypeStruct(outgoing.shape, jnp.bfloat16),
            jax.ShapeDtypeStruct(cotangent.shape, jnp.bfloat16),
            jax.ShapeDtypeStruct((rank, features), jnp.float32),
            jax.ShapeDtypeStruct((rank, columns), jnp.float32),
        ],
        scratch_shapes=[
            pltpu.VMEM((cores, *hidden_part.shape), jnp.float32),
            *pieces(near, far),
            *pieces(near, far),
            *pieces(far),
            *pieces(far),
            *pieces(near, far),
            *semaphores(MOVES),
            *semaphores(cores),
            *semaphores(2, near),
            *semaphores(2, far),
            *semaphores(2, far),
            *semaphores(2, near),
        ],
        compiler_params=pltpu.CompilerParams(
            collective_id=0, has_side_effects=True, vmem_limit_bytes=48 * 2**20
        ),
        cost_estimate=pl.CostEstimate(
            flops=4 * rank * cotangent.size, bytes_accessed=8 * cotangent.size, transcendentals=0
        ),
    )(outgoing, hidden_part, grad_down_part, up_weight, cotangent)


def on_device(
    queries,
    key_value_pairs,
    document_numbers,
    destinations,
    adapter_down_weight,
    adapter_up_weight,
    cotangent,
):
    token_rows = queries.shape[0]
    replica_list = lax.axis_size("dp")
    own_index = lax.axis_index("dp")
    gradient_scale = ADAPTER_SCALE / math.sqrt(token_rows * replica_list)
    partial_feedback = lax.dot_general(
        adapter_up_weight, cotangent, (((1,), (1,)), ((), ())), preferred_element_type=jnp.float32
    )
    feedback_signal = lax.psum(partial_feedback, "tensor").astype(jnp.bfloat16)

    doc_ids = jnp.arange(NDOC, dtype=jnp.int32)
    lengths = jnp.sum((document_numbers[:, None] == doc_ids).astype(jnp.int32), axis=0)
    starts = jnp.sum((document_numbers[:, None] < doc_ids).astype(jnp.int32), axis=0)
    partners = jnp.bitwise_xor(
        own_index, jnp.array([replica_list >> k + 1 for k in range(MOVES)], jnp.int32)
    )
    chosen = destinations[0][None, :] == partners[:, None]
    sent_start = jnp.sum(jnp.where(chosen, starts, 0), axis=1)
    sent_length = jnp.sum(jnp.where(chosen, lengths, 0), axis=1)
    offsets = jnp.arange(CAP, dtype=jnp.int32)[None, :]
    targets = jnp.where(
        offsets < sent_length[:, None], sent_start[:, None] + offsets, -1
    ).reshape(MOVES * CAP)
    blocks = token_rows // TILE
    first_document = document_numbers.reshape(blocks, TILE)[:, 0]
    first_row = jnp.sum(
        (document_numbers[None, :] < first_document[:, None]).astype(jnp.int32), axis=1
    )
    tiles = jnp.arange(1, blocks + 1, dtype=jnp.int32) - first_row // TILE

    outgoing, hidden_part, grad_down_part = attend_all(
        queries, key_value_pairs[:, 0], key_value_pairs[:, 1], document_numbers, tiles, targets,
        adapter_down_weight, feedback_signal, gradient_scale,
    )
    arrived_out, adapter_output, grad_down, grad_up = exchange(
        outgoing, hidden_part, grad_down_part, adapter_up_weight, cotangent, gradient_scale
    )
    return (arrived_out, adapter_output, grad_down.T, grad_up)


def solution(mesh):
    placed = (
        P("dp", "tensor"),
        P("dp", None, "tensor"),
        P("dp"),
        P("dp", None),
        P("tensor", None),
        P(None, "tensor"),
        P("dp", "tensor"),
    )
    return jax.shard_map(
        on_device,
        mesh=mesh,
        in_specs=placed,
        out_specs=(P("dp", "tensor"), P("dp", "tensor"), P("tensor", None), P(None, "tensor")),
        check_vma=False,
    )
```

```python
import functools
import math

import jax
import jax.numpy as jnp
from jax import lax
from jax.experimental import pallas as pl
from jax.experimental.pallas import tpu as pltpu
from jax.sharding import PartitionSpec as P

HEAD_SIZE = 128
NDOC = 12
MOVES = 4
CAP = 64
TILE = 128
HEADS_PER_DOT = 4

ADAPTER_SCALE = 2.0
MASKED_SCORE = -1e30
EXP2_SCALE = HEAD_SIZE ** (-0.5) * math.log2(math.e)


def attention_kernel(
    gradient_scale, tiles_ref, query_ref, key_ref, value_ref, doc_col_ref, doc_row_ref, target_ref,
    down_ref, feedback_ref, outgoing_ref, hidden_ref, grad_ref, attention_ref,
):
    group, block = pl.program_id(0), pl.program_id(1)
    blocks = attention_ref.shape[0] // TILE
    heads = query_ref.shape[1] // HEAD_SIZE

    def attend(count):
        width = count * TILE
        start = pl.multiple_of((block + 1 - count) * TILE, TILE)
        keys = key_ref[pl.ds(start, width), :]
        values = jnp.concatenate(
            [value_ref[pl.ds(start, width), :], jnp.ones((width, HEAD_SIZE), jnp.bfloat16)], axis=1
        )
        rows = lax.broadcasted_iota(jnp.int32, (TILE, width), 0) + block * TILE
        columns = lax.broadcasted_iota(jnp.int32, (TILE, width), 1) + start
        same = doc_col_ref[...] == doc_row_ref[:, pl.ds(start, width)]
        bias = jnp.where(same & (rows >= columns), 0.0, MASKED_SCORE)
        for first in range(0, heads, HEADS_PER_DOT):
            picked = range(first, min(first + HEADS_PER_DOT, heads))
            stacked = jnp.concatenate(
                [query_ref[:, h * HEAD_SIZE : (h + 1) * HEAD_SIZE] for h in picked], axis=0
            )
            scores = lax.dot_general(
                stacked, keys, (((1,), (1,)), ((), ())), preferred_element_type=jnp.float32
            )
            scores = scores.reshape(len(picked), TILE, width) * EXP2_SCALE + bias[None]
            row_max = jnp.max(scores, axis=2, keepdims=True)
            weights = jnp.exp2(scores - row_max).astype(jnp.bfloat16)
            product = jnp.dot(
                weights.reshape(len(picked) * TILE, width), values,
                preferred_element_type=jnp.float32,
            )
            result = (product[:, :HEAD_SIZE] / product[:, HEAD_SIZE:]).astype(jnp.bfloat16)
            for at, h in enumerate(picked):
                attention_ref[
                    pl.ds(pl.multiple_of(block * TILE, TILE), TILE),
                    h * HEAD_SIZE : (h + 1) * HEAD_SIZE,
                ] = result[at * TILE : (at + 1) * TILE]

    for count in range(1, blocks + 1):
        pl.when(tiles_ref[block] == count)(functools.partial(attend, count))

    @pl.when(block == blocks - 1)
    def _():
        attention = attention_ref[...]
        moved = lax.broadcasted_iota(jnp.int32, (MOVES * CAP, attention.shape[0]), 1)
        pick = jnp.where(moved == target_ref[...], 1.0, 0.0).astype(jnp.bfloat16)
        outgoing_ref[...] = jnp.dot(
            pick, attention, preferred_element_type=jnp.float32
        ).astype(jnp.bfloat16)
        part = lax.dot_general(
            attention, down_ref[...], (((1,), (1,)), ((), ())), preferred_element_type=jnp.float32
        )

        @pl.when(group == 0)
        def _():
            hidden_ref[...] = part

        @pl.when(group > 0)
        def _():
            hidden_ref[...] += part

        grad_ref[...] = gradient_scale * jnp.dot(
            feedback_ref[...], attention, preferred_element_type=jnp.float32
        )


def attend_all(
    queries, keys, values, documents, tiles, targets, down_weight, feedback, gradient_scale
):
    rows, features = queries.shape
    groups = keys.shape[1] // HEAD_SIZE
    width = features // groups
    rank = down_weight.shape[1]
    blocks = rows // TILE
    grid_spec = pltpu.PrefetchScalarGridSpec(
        num_scalar_prefetch=1,
        grid=(groups, blocks),
        in_specs=[
            pl.BlockSpec((TILE, width), lambda g, i, t: (i, g)),
            pl.BlockSpec((rows, HEAD_SIZE), lambda g, i, t: (0, g)),
            pl.BlockSpec((rows, HEAD_SIZE), lambda g, i, t: (0, g)),
            pl.BlockSpec((TILE, 1), lambda g, i, t: (i, 0)),
            pl.BlockSpec((1, rows), lambda g, i, t: (0, 0)),
            pl.BlockSpec((MOVES * CAP, 1), lambda g, i, t: (0, 0)),
            pl.BlockSpec((rank, width), lambda g, i, t: (0, g)),
            pl.BlockSpec((rank, rows), lambda g, i, t: (0, 0)),
        ],
        out_specs=[
            pl.BlockSpec((MOVES * CAP, width), lambda g, i, t: (0, g)),
            pl.BlockSpec((rows, rank), lambda g, i, t: (0, 0)),
            pl.BlockSpec((rank, width), lambda g, i, t: (0, g)),
        ],
        scratch_shapes=[pltpu.VMEM((rows, width), jnp.bfloat16)],
    )
    return pl.pallas_call(
        functools.partial(attention_kernel, gradient_scale),
        grid_spec=grid_spec,
        out_shape=[
            jax.ShapeDtypeStruct((MOVES * CAP, features), jnp.bfloat16),
            jax.ShapeDtypeStruct((rows, rank), jnp.float32),
            jax.ShapeDtypeStruct((rank, features), jnp.float32),
        ],
        compiler_params=pltpu.CompilerParams(vmem_limit_bytes=40 * 2**20),
        cost_estimate=pl.CostEstimate(
            flops=3 * rows * rows * features, bytes_accessed=4 * rows * features,
            transcendentals=rows * rows * features // (2 * HEAD_SIZE),
        ),
    )(
        tiles, queries, keys, values, documents[:, None], documents[None, :], targets[:, None],
        down_weight.T, feedback,
    )


def exchange_kernel(
    sizes, gradient_scale, outgoing_ref, hidden_ref, down_part_ref, up_ref, cotangent_ref,
    arrived_ref, output_ref, grad_down_ref, grad_up_ref,
    hidden_in, parts0, parts1, near0, near1, sums0, sums1, far0, far1, whole0, whole1,
    move_send, move_recv, hidden_send, hidden_recv, near_send, near_recv, far_send, far_recv,
    back_send, back_recv, full_send, full_recv,
):
    near, far, cores, lanes = sizes
    replicas = near * far
    own = lax.axis_index("dp")
    core = lax.axis_index("tensor")
    mine, level = lax.rem(own, near), own // near
    columns_out = output_ref.shape[1]

    def near_peer(step):
        return lax.rem(mine + step, near)

    def far_peer(step):
        return lax.rem(level + step, far)

    def at_near(step):
        return {"dp": level * near + near_peer(step)}

    def at_far(step):
        return {"dp": far_peer(step) * near + mine}

    def at_core(step):
        return {"tensor": lax.rem(core + step, cores)}

    devices = [at_near(d) for d in range(1, near)] + [at_far(d) for d in range(1, far)]
    devices += [at_core(d) for d in range(1, cores)]
    barrier = pltpu.get_barrier_semaphore()
    for device in devices:
        pl.semaphore_signal(barrier, inc=1, device_id=device, device_id_type=pl.DeviceIdType.MESH)
    pl.semaphore_wait(barrier, len(devices))

    started = []

    def send(source, target, send_sem, recv_sem, device):
        copy = pltpu.make_async_remote_copy(
            src_ref=source, dst_ref=target, send_sem=send_sem, recv_sem=recv_sem,
            device_id=device, device_id_type=pl.DeviceIdType.MESH,
        )
        copy.start()
        started.append(copy)
        return copy

    def move(slots):
        copies = []
        for k in slots:
            bit = replicas >> k + 1
            partner = own + bit - 2 * bit * lax.rem(own // bit, 2)
            rows = pl.ds(k * CAP, CAP)
            copies.append(
                send(
                    outgoing_ref.at[rows], arrived_ref.at[rows], move_send.at[k], move_recv.at[k],
                    {"dp": partner},
                )
            )
        return copies

    far_moves = [k for k in range(MOVES) if replicas >> k + 1 >= near]
    near_moves = [k for k in range(MOVES) if replicas >> k + 1 < near]
    move_copies = move(far_moves)
    hidden_copies = [
        send(hidden_ref, hidden_in.at[d], hidden_send.at[d], hidden_recv.at[d], at_core(d))
        for d in range(1, cores)
    ]

    def fill(parts, value):
        width = parts.shape[3]
        for chunk in range(replicas):
            row, lane = chunk // lanes, chunk % lanes
            have = max(0, min(width, value.shape[1] - lane * width))
            slot = parts.at[chunk // far, chunk % far]
            if have < width:
                slot[...] = jnp.zeros((16, width), jnp.bfloat16)
            if have:
                slot[:, :have] = value[
                    row * 16 : (row + 1) * 16, lane * width : lane * width + have
                ].astype(jnp.bfloat16)

    def scatter_near(at, parts, arrivals):
        return [
            send(
                parts.at[near_peer(d)], arrivals.at[d], near_send.at[at, d], near_recv.at[at, d],
                at_near(d),
            )
            for d in range(1, near)
        ]

    fill(parts0, down_part_ref)
    near_copies0 = scatter_near(0, parts0, near0)

    total = hidden_ref[...]
    for d, copy in enumerate(hidden_copies):
        copy.wait_recv()
        total = total + hidden_in[d + 1]
    hidden = total.astype(jnp.bfloat16)
    hidden_turned = total.T.astype(jnp.bfloat16)
    fill(
        parts1,
        gradient_scale
        * jnp.dot(hidden_turned, cotangent_ref[...], preferred_element_type=jnp.float32),
    )
    near_copies1 = scatter_near(1, parts1, near1)

    step = 640 if columns_out % 640 == 0 else 128
    for first in range(0, columns_out, step):
        output_ref[:, first : first + step] = (
            ADAPTER_SCALE
            * jnp.dot(
                hidden, up_ref[:, first : first + step], preferred_element_type=jnp.float32
            )
        ).astype(jnp.bfloat16)

    def sum_near(copies, parts, arrivals, sums):
        value = parts[mine].astype(jnp.float32)
        for d, copy in enumerate(copies):
            copy.wait_recv()
            value = value + arrivals[d + 1].astype(jnp.float32)
        sums[...] = value.astype(jnp.bfloat16)

    def scatter_far(at, sums, arrivals):
        return [
            send(
                sums.at[far_peer(d)], arrivals.at[d], far_send.at[at, d], far_recv.at[at, d],
                at_far(d),
            )
            for d in range(1, far)
        ]

    def sum_far(copies, sums, arrivals, whole):
        value = sums[level].astype(jnp.float32)
        for d, copy in enumerate(copies):
            copy.wait_recv()
            value = value + arrivals[d + 1].astype(jnp.float32)
        whole[mine, level] = value.astype(jnp.bfloat16)

    def gather_far(at, whole):
        return [
            send(
                whole.at[mine, level], whole.at[mine, level], back_send.at[at, d],
                back_recv.at[at, d], at_far(d),
            )
            for d in range(1, far)
        ]

    def gather_near(at, copies, whole):
        for copy in copies:
            copy.wait_recv()
        return [
            send(
                whole.at[mine], whole.at[mine], full_send.at[at, d], full_recv.at[at, d],
                at_near(d),
            )
            for d in range(1, near)
        ]

    def give(copies, whole, target):
        for copy in copies:
            copy.wait_recv()
        width = whole.shape[3]
        for chunk in range(replicas):
            row, lane = chunk // lanes, chunk % lanes
            have = max(0, min(width, target.shape[1] - lane * width))
            if have:
                target[row * 16 : (row + 1) * 16, lane * width : lane * width + have] = whole[
                    chunk // far, chunk % far
                ][:, :have].astype(jnp.float32)

    sum_near(near_copies0, parts0, near0, sums0)
    far_copies0 = scatter_far(0, sums0, far0)
    sum_near(near_copies1, parts1, near1, sums1)
    far_copies1 = scatter_far(1, sums1, far1)
    move_copies += move(near_moves)
    sum_far(far_copies0, sums0, far0, whole0)
    back_copies0 = gather_far(0, whole0)
    sum_far(far_copies1, sums1, far1, whole1)
    back_copies1 = gather_far(1, whole1)
    full_copies0 = gather_near(0, back_copies0, whole0)
    full_copies1 = gather_near(1, back_copies1, whole1)
    give(full_copies0, whole0, grad_down_ref)
    give(full_copies1, whole1, grad_up_ref)
    for copy in move_copies:
        copy.wait_recv()
    for copy in started:
        copy.wait_send()


def exchange(outgoing, hidden_part, grad_down_part, up_weight, cotangent, gradient_scale):
    replicas, cores = lax.axis_size("dp"), lax.axis_size("tensor")
    near = 1 << replicas.bit_length() // 2
    far = replicas // near
    rank, features = grad_down_part.shape
    columns = cotangent.shape[1]
    lanes = replicas * 16 // rank
    widths = [-(-size // (lanes * 128)) * 128 for size in (features, columns)]

    def pieces(*lead):
        return [pltpu.VMEM((*lead, 16, width), jnp.bfloat16) for width in widths]

    def semaphores(*shape):
        return [pltpu.SemaphoreType.DMA(shape), pltpu.SemaphoreType.DMA(shape)]

    vmem = pl.BlockSpec(memory_space=pltpu.VMEM)
    hbm = pl.BlockSpec(memory_space=pl.ANY)
    return pl.pallas_call(
        functools.partial(exchange_kernel, (near, far, cores, lanes), gradient_scale),
        in_specs=[vmem, vmem, vmem, vmem, vmem],
        out_specs=[hbm, vmem, vmem, vmem],
        out_shape=[
            jax.ShapeDtypeStruct(outgoing.shape, jnp.bfloat16),
            jax.ShapeDtypeStruct(cotangent.shape, jnp.bfloat16),
            jax.ShapeDtypeStruct((rank, features), jnp.float32),
            jax.ShapeDtypeStruct((rank, columns), jnp.float32),
        ],
        scratch_shapes=[
            pltpu.VMEM((cores, *hidden_part.shape), jnp.float32),
            *pieces(near, far),
            *pieces(near, far),
            *pieces(far),
            *pieces(far),
            *pieces(near, far),
            *semaphores(MOVES),
            *semaphores(cores),
            *semaphores(2, near),
            *semaphores(2, far),
            *semaphores(2, far),
            *semaphores(2, near),
        ],
        compiler_params=pltpu.CompilerParams(
            collective_id=0, has_side_effects=True, vmem_limit_bytes=48 * 2**20
        ),
        cost_estimate=pl.CostEstimate(
            flops=4 * rank * cotangent.size, bytes_accessed=8 * cotangent.size, transcendentals=0
        ),
    )(outgoing, hidden_part, grad_down_part, up_weight, cotangent)


def on_device(
    queries,
    key_value_pairs,
    document_numbers,
    destinations,
    adapter_down_weight,
    adapter_up_weight,
    cotangent,
):
    token_rows = queries.shape[0]
    replica_list = lax.axis_size("dp")
    own_index = lax.axis_index("dp")
    gradient_scale = ADAPTER_SCALE / math.sqrt(token_rows * replica_list)
    partial_feedback = lax.dot_general(
        adapter_up_weight, cotangent, (((1,), (1,)), ((), ())), preferred_element_type=jnp.float32
    )
    feedback_signal = lax.psum(partial_feedback, "tensor").astype(jnp.bfloat16)

    doc_ids = jnp.arange(NDOC, dtype=jnp.int32)
    lengths = jnp.sum((document_numbers[:, None] == doc_ids).astype(jnp.int32), axis=0)
    starts = jnp.sum((document_numbers[:, None] < doc_ids).astype(jnp.int32), axis=0)
    partners = jnp.bitwise_xor(
        own_index, jnp.array([replica_list >> k + 1 for k in range(MOVES)], jnp.int32)
    )
    chosen = destinations[0][None, :] == partners[:, None]
    sent_start = jnp.sum(jnp.where(chosen, starts, 0), axis=1)
    sent_length = jnp.sum(jnp.where(chosen, lengths, 0), axis=1)
    offsets = jnp.arange(CAP, dtype=jnp.int32)[None, :]
    targets = jnp.where(
        offsets < sent_length[:, None], sent_start[:, None] + offsets, -1
    ).reshape(MOVES * CAP)
    blocks = token_rows // TILE
    first_document = document_numbers.reshape(blocks, TILE)[:, 0]
    first_row = jnp.sum(
        (document_numbers[None, :] < first_document[:, None]).astype(jnp.int32), axis=1
    )
    tiles = jnp.arange(1, blocks + 1, dtype=jnp.int32) - first_row // TILE

    outgoing, hidden_part, grad_down_part = attend_all(
        queries, key_value_pairs[:, 0], key_value_pairs[:, 1], document_numbers, tiles, targets,
        adapter_down_weight, feedback_signal, gradient_scale,
    )
    arrived_out, adapter_output, grad_down, grad_up = exchange(
        outgoing, hidden_part, grad_down_part, adapter_up_weight, cotangent, gradient_scale
    )
    return (arrived_out, adapter_output, grad_down.T, grad_up)


def solution(mesh):
    placed = (
        P("dp", "tensor"),
        P("dp", None, "tensor"),
        P("dp"),
        P("dp", None),
        P("tensor", None),
        P(None, "tensor"),
        P("dp", "tensor"),
    )
    return jax.shard_map(
        on_device,
        mesh=mesh,
        in_specs=placed,
        out_specs=(P("dp", "tensor"), P("dp", "tensor"), P("tensor", None), P(None, "tensor")),
        check_vma=False,
    )
```

```python
import functools
import math

import jax
import jax.numpy as jnp
from jax import lax
from jax.experimental import pallas as pl
from jax.experimental.pallas import tpu as pltpu
from jax.sharding import PartitionSpec as P

HEAD_SIZE = 128
NDOC = 12
MOVES = 4
CAP = 64
TILE = 128
HEADS_PER_DOT = 8

ADAPTER_SCALE = 2.0
MASKED_SCORE = -1e30
EXP2_SCALE = HEAD_SIZE ** (-0.5) * math.log2(math.e)


def attention_kernel(
    gradient_scale, tiles_ref, query_ref, key_ref, value_ref, doc_col_ref, doc_row_ref, target_ref,
    down_ref, feedback_ref, outgoing_ref, hidden_ref, grad_ref, attention_ref,
):
    group, block = pl.program_id(0), pl.program_id(1)
    blocks = attention_ref.shape[0] // TILE
    heads = query_ref.shape[1] // HEAD_SIZE

    def attend(count):
        width = count * TILE
        start = pl.multiple_of((block + 1 - count) * TILE, TILE)
        keys = key_ref[pl.ds(start, width), :]
        values = jnp.concatenate(
            [value_ref[pl.ds(start, width), :], jnp.ones((width, HEAD_SIZE), jnp.bfloat16)], axis=1
        )
        rows = lax.broadcasted_iota(jnp.int32, (TILE, width), 0) + block * TILE
        columns = lax.broadcasted_iota(jnp.int32, (TILE, width), 1) + start
        same = doc_col_ref[...] == doc_row_ref[:, pl.ds(start, width)]
        bias = jnp.where(same & (rows >= columns), 0.0, MASKED_SCORE)
        for first in range(0, heads, HEADS_PER_DOT):
            picked = range(first, min(first + HEADS_PER_DOT, heads))
            stacked = jnp.concatenate(
                [query_ref[:, h * HEAD_SIZE : (h + 1) * HEAD_SIZE] for h in picked], axis=0
            )
            scores = lax.dot_general(
                stacked, keys, (((1,), (1,)), ((), ())), preferred_element_type=jnp.float32
            )
            scores = scores.reshape(len(picked), TILE, width) * EXP2_SCALE + bias[None]
            row_max = jnp.max(scores, axis=2, keepdims=True)
            weights = jnp.exp2(scores - row_max).astype(jnp.bfloat16)
            product = jnp.dot(
                weights.reshape(len(picked) * TILE, width), values,
                preferred_element_type=jnp.float32,
            )
            result = (product[:, :HEAD_SIZE] / product[:, HEAD_SIZE:]).astype(jnp.bfloat16)
            for at, h in enumerate(picked):
                attention_ref[
                    pl.ds(pl.multiple_of(block * TILE, TILE), TILE),
                    h * HEAD_SIZE : (h + 1) * HEAD_SIZE,
                ] = result[at * TILE : (at + 1) * TILE]

    for count in range(1, blocks + 1):
        pl.when(tiles_ref[block] == count)(functools.partial(attend, count))

    @pl.when(block == blocks - 1)
    def _():
        attention = attention_ref[...]
        moved = lax.broadcasted_iota(jnp.int32, (MOVES * CAP, attention.shape[0]), 1)
        pick = jnp.where(moved == target_ref[...], 1.0, 0.0).astype(jnp.bfloat16)
        outgoing_ref[...] = jnp.dot(
            pick, attention, preferred_element_type=jnp.float32
        ).astype(jnp.bfloat16)
        part = lax.dot_general(
            attention, down_ref[...], (((1,), (1,)), ((), ())), preferred_element_type=jnp.float32
        )

        @pl.when(group == 0)
        def _():
            hidden_ref[...] = part

        @pl.when(group > 0)
        def _():
            hidden_ref[...] += part

        grad_ref[...] = gradient_scale * jnp.dot(
            feedback_ref[...], attention, preferred_element_type=jnp.float32
        )


def attend_all(
    queries, keys, values, documents, tiles, targets, down_weight, feedback, gradient_scale
):
    rows, features = queries.shape
    groups = keys.shape[1] // HEAD_SIZE
    width = features // groups
    rank = down_weight.shape[1]
    blocks = rows // TILE
    grid_spec = pltpu.PrefetchScalarGridSpec(
        num_scalar_prefetch=1,
        grid=(groups, blocks),
        in_specs=[
            pl.BlockSpec((TILE, width), lambda g, i, t: (i, g)),
            pl.BlockSpec((rows, HEAD_SIZE), lambda g, i, t: (0, g)),
            pl.BlockSpec((rows, HEAD_SIZE), lambda g, i, t: (0, g)),
            pl.BlockSpec((TILE, 1), lambda g, i, t: (i, 0)),
            pl.BlockSpec((1, rows), lambda g, i, t: (0, 0)),
            pl.BlockSpec((MOVES * CAP, 1), lambda g, i, t: (0, 0)),
            pl.BlockSpec((rank, width), lambda g, i, t: (0, g)),
            pl.BlockSpec((rank, rows), lambda g, i, t: (0, 0)),
        ],
        out_specs=[
            pl.BlockSpec((MOVES * CAP, width), lambda g, i, t: (0, g)),
            pl.BlockSpec((rows, rank), lambda g, i, t: (0, 0)),
            pl.BlockSpec((rank, width), lambda g, i, t: (0, g)),
        ],
        scratch_shapes=[pltpu.VMEM((rows, width), jnp.bfloat16)],
    )
    return pl.pallas_call(
        functools.partial(attention_kernel, gradient_scale),
        grid_spec=grid_spec,
        out_shape=[
            jax.ShapeDtypeStruct((MOVES * CAP, features), jnp.bfloat16),
            jax.ShapeDtypeStruct((rows, rank), jnp.float32),
            jax.ShapeDtypeStruct((rank, features), jnp.float32),
        ],
        compiler_params=pltpu.CompilerParams(vmem_limit_bytes=40 * 2**20),
        cost_estimate=pl.CostEstimate(
            flops=3 * rows * rows * features, bytes_accessed=4 * rows * features,
            transcendentals=rows * rows * features // (2 * HEAD_SIZE),
        ),
    )(
        tiles, queries, keys, values, documents[:, None], documents[None, :], targets[:, None],
        down_weight.T, feedback,
    )


def exchange_kernel(
    sizes, gradient_scale, outgoing_ref, hidden_ref, down_part_ref, up_ref, cotangent_ref,
    arrived_ref, output_ref, grad_down_ref, grad_up_ref,
    hidden_in, parts0, parts1, near0, near1, sums0, sums1, far0, far1, whole0, whole1,
    move_send, move_recv, hidden_send, hidden_recv, near_send, near_recv, far_send, far_recv,
    back_send, back_recv, full_send, full_recv,
):
    near, far, cores, lanes = sizes
    replicas = near * far
    own = lax.axis_index("dp")
    core = lax.axis_index("tensor")
    mine, level = lax.rem(own, near), own // near
    columns_out = output_ref.shape[1]

    def near_peer(step):
        return lax.rem(mine + step, near)

    def far_peer(step):
        return lax.rem(level + step, far)

    def at_near(step):
        return {"dp": level * near + near_peer(step)}

    def at_far(step):
        return {"dp": far_peer(step) * near + mine}

    def at_core(step):
        return {"tensor": lax.rem(core + step, cores)}

    devices = [at_near(d) for d in range(1, near)] + [at_far(d) for d in range(1, far)]
    devices += [at_core(d) for d in range(1, cores)]
    barrier = pltpu.get_barrier_semaphore()
    for device in devices:
        pl.semaphore_signal(barrier, inc=1, device_id=device, device_id_type=pl.DeviceIdType.MESH)
    pl.semaphore_wait(barrier, len(devices))

    started = []

    def send(source, target, send_sem, recv_sem, device):
        copy = pltpu.make_async_remote_copy(
            src_ref=source, dst_ref=target, send_sem=send_sem, recv_sem=recv_sem,
            device_id=device, device_id_type=pl.DeviceIdType.MESH,
        )
        copy.start()
        started.append(copy)
        return copy

    def move(slots):
        copies = []
        for k in slots:
            bit = replicas >> k + 1
            partner = own + bit - 2 * bit * lax.rem(own // bit, 2)
            rows = pl.ds(k * CAP, CAP)
            copies.append(
                send(
                    outgoing_ref.at[rows], arrived_ref.at[rows], move_send.at[k], move_recv.at[k],
                    {"dp": partner},
                )
            )
        return copies

    far_moves = [k for k in range(MOVES) if replicas >> k + 1 >= near]
    near_moves = [k for k in range(MOVES) if replicas >> k + 1 < near]
    move_copies = move(far_moves)
    hidden_copies = [
        send(hidden_ref, hidden_in.at[d], hidden_send.at[d], hidden_recv.at[d], at_core(d))
        for d in range(1, cores)
    ]

    def fill(parts, value):
        width = parts.shape[3]
        for chunk in range(replicas):
            row, lane = chunk // lanes, chunk % lanes
            have = max(0, min(width, value.shape[1] - lane * width))
            slot = parts.at[chunk // far, chunk % far]
            if have < width:
                slot[...] = jnp.zeros((16, width), jnp.bfloat16)
            if have:
                slot[:, :have] = value[
                    row * 16 : (row + 1) * 16, lane * width : lane * width + have
                ].astype(jnp.bfloat16)

    def scatter_near(at, parts, arrivals):
        return [
            send(
                parts.at[near_peer(d)], arrivals.at[d], near_send.at[at, d], near_recv.at[at, d],
                at_near(d),
            )
            for d in range(1, near)
        ]

    fill(parts0, down_part_ref)
    near_copies0 = scatter_near(0, parts0, near0)

    total = hidden_ref[...]
    for d, copy in enumerate(hidden_copies):
        copy.wait_recv()
        total = total + hidden_in[d + 1]
    hidden = total.astype(jnp.bfloat16)
    hidden_turned = total.T.astype(jnp.bfloat16)
    fill(
        parts1,
        gradient_scale
        * jnp.dot(hidden_turned, cotangent_ref[...], preferred_element_type=jnp.float32),
    )
    near_copies1 = scatter_near(1, parts1, near1)

    step = 640 if columns_out % 640 == 0 else 128
    for first in range(0, columns_out, step):
        output_ref[:, first : first + step] = (
            ADAPTER_SCALE
            * jnp.dot(
                hidden, up_ref[:, first : first + step], preferred_element_type=jnp.float32
            )
        ).astype(jnp.bfloat16)

    def sum_near(copies, parts, arrivals, sums):
        value = parts[mine].astype(jnp.float32)
        for d, copy in enumerate(copies):
            copy.wait_recv()
            value = value + arrivals[d + 1].astype(jnp.float32)
        sums[...] = value.astype(jnp.bfloat16)

    def scatter_far(at, sums, arrivals):
        return [
            send(
                sums.at[far_peer(d)], arrivals.at[d], far_send.at[at, d], far_recv.at[at, d],
                at_far(d),
            )
            for d in range(1, far)
        ]

    def sum_far(copies, sums, arrivals, whole):
        value = sums[level].astype(jnp.float32)
        for d, copy in enumerate(copies):
            copy.wait_recv()
            value = value + arrivals[d + 1].astype(jnp.float32)
        whole[mine, level] = value.astype(jnp.bfloat16)

    def gather_far(at, whole):
        return [
            send(
                whole.at[mine, level], whole.at[mine, level], back_send.at[at, d],
                back_recv.at[at, d], at_far(d),
            )
            for d in range(1, far)
        ]

    def gather_near(at, copies, whole):
        for copy in copies:
            copy.wait_recv()
        return [
            send(
                whole.at[mine], whole.at[mine], full_send.at[at, d], full_recv.at[at, d],
                at_near(d),
            )
            for d in range(1, near)
        ]

    def give(copies, whole, target):
        for copy in copies:
            copy.wait_recv()
        width = whole.shape[3]
        for chunk in range(replicas):
            row, lane = chunk // lanes, chunk % lanes
            have = max(0, min(width, target.shape[1] - lane * width))
            if have:
                target[row * 16 : (row + 1) * 16, lane * width : lane * width + have] = whole[
                    chunk // far, chunk % far
                ][:, :have].astype(jnp.float32)

    sum_near(near_copies0, parts0, near0, sums0)
    far_copies0 = scatter_far(0, sums0, far0)
    sum_near(near_copies1, parts1, near1, sums1)
    far_copies1 = scatter_far(1, sums1, far1)
    move_copies += move(near_moves)
    sum_far(far_copies0, sums0, far0, whole0)
    back_copies0 = gather_far(0, whole0)
    sum_far(far_copies1, sums1, far1, whole1)
    back_copies1 = gather_far(1, whole1)
    full_copies0 = gather_near(0, back_copies0, whole0)
    full_copies1 = gather_near(1, back_copies1, whole1)
    give(full_copies0, whole0, grad_down_ref)
    give(full_copies1, whole1, grad_up_ref)
    for copy in move_copies:
        copy.wait_recv()
    for copy in started:
        copy.wait_send()


def exchange(outgoing, hidden_part, grad_down_part, up_weight, cotangent, gradient_scale):
    replicas, cores = lax.axis_size("dp"), lax.axis_size("tensor")
    near = 1 << replicas.bit_length() // 2
    far = replicas // near
    rank, features = grad_down_part.shape
    columns = cotangent.shape[1]
    lanes = replicas * 16 // rank
    widths = [-(-size // (lanes * 128)) * 128 for size in (features, columns)]

    def pieces(*lead):
        return [pltpu.VMEM((*lead, 16, width), jnp.bfloat16) for width in widths]

    def semaphores(*shape):
        return [pltpu.SemaphoreType.DMA(shape), pltpu.SemaphoreType.DMA(shape)]

    vmem = pl.BlockSpec(memory_space=pltpu.VMEM)
    hbm = pl.BlockSpec(memory_space=pl.ANY)
    return pl.pallas_call(
        functools.partial(exchange_kernel, (near, far, cores, lanes), gradient_scale),
        in_specs=[vmem, vmem, vmem, vmem, vmem],
        out_specs=[hbm, vmem, vmem, vmem],
        out_shape=[
            jax.ShapeDtypeStruct(outgoing.shape, jnp.bfloat16),
            jax.ShapeDtypeStruct(cotangent.shape, jnp.bfloat16),
            jax.ShapeDtypeStruct((rank, features), jnp.float32),
            jax.ShapeDtypeStruct((rank, columns), jnp.float32),
        ],
        scratch_shapes=[
            pltpu.VMEM((cores, *hidden_part.shape), jnp.float32),
            *pieces(near, far),
            *pieces(near, far),
            *pieces(far),
            *pieces(far),
            *pieces(near, far),
            *semaphores(MOVES),
            *semaphores(cores),
            *semaphores(2, near),
            *semaphores(2, far),
            *semaphores(2, far),
            *semaphores(2, near),
        ],
        compiler_params=pltpu.CompilerParams(
            collective_id=0, has_side_effects=True, vmem_limit_bytes=48 * 2**20
        ),
        cost_estimate=pl.CostEstimate(
            flops=4 * rank * cotangent.size, bytes_accessed=8 * cotangent.size, transcendentals=0
        ),
    )(outgoing, hidden_part, grad_down_part, up_weight, cotangent)


def on_device(
    queries,
    key_value_pairs,
    document_numbers,
    destinations,
    adapter_down_weight,
    adapter_up_weight,
    cotangent,
):
    token_rows = queries.shape[0]
    replica_list = lax.axis_size("dp")
    own_index = lax.axis_index("dp")
    gradient_scale = ADAPTER_SCALE / math.sqrt(token_rows * replica_list)
    partial_feedback = lax.dot_general(
        adapter_up_weight, cotangent, (((1,), (1,)), ((), ())), preferred_element_type=jnp.float32
    )
    feedback_signal = lax.psum(partial_feedback, "tensor").astype(jnp.bfloat16)

    doc_ids = jnp.arange(NDOC, dtype=jnp.int32)
    lengths = jnp.sum((document_numbers[:, None] == doc_ids).astype(jnp.int32), axis=0)
    starts = jnp.sum((document_numbers[:, None] < doc_ids).astype(jnp.int32), axis=0)
    partners = jnp.bitwise_xor(
        own_index, jnp.array([replica_list >> k + 1 for k in range(MOVES)], jnp.int32)
    )
    chosen = destinations[0][None, :] == partners[:, None]
    sent_start = jnp.sum(jnp.where(chosen, starts, 0), axis=1)
    sent_length = jnp.sum(jnp.where(chosen, lengths, 0), axis=1)
    offsets = jnp.arange(CAP, dtype=jnp.int32)[None, :]
    targets = jnp.where(
        offsets < sent_length[:, None], sent_start[:, None] + offsets, -1
    ).reshape(MOVES * CAP)
    blocks = token_rows // TILE
    first_document = document_numbers.reshape(blocks, TILE)[:, 0]
    first_row = jnp.sum(
        (document_numbers[None, :] < first_document[:, None]).astype(jnp.int32), axis=1
    )
    tiles = jnp.arange(1, blocks + 1, dtype=jnp.int32) - first_row // TILE

    outgoing, hidden_part, grad_down_part = attend_all(
        queries, key_value_pairs[:, 0], key_value_pairs[:, 1], document_numbers, tiles, targets,
        adapter_down_weight, feedback_signal, gradient_scale,
    )
    arrived_out, adapter_output, grad_down, grad_up = exchange(
        outgoing, hidden_part, grad_down_part, adapter_up_weight, cotangent, gradient_scale
    )
    return (arrived_out, adapter_output, grad_down.T, grad_up)


def solution(mesh):
    placed = (
        P("dp", "tensor"),
        P("dp", None, "tensor"),
        P("dp"),
        P("dp", None),
        P("tensor", None),
        P(None, "tensor"),
        P("dp", "tensor"),
    )
    return jax.shard_map(
        on_device,
        mesh=mesh,
        in_specs=placed,
        out_specs=(P("dp", "tensor"), P("dp", "tensor"), P("tensor", None), P(None, "tensor")),
        check_vma=False,
    )
```
